128 devices in a mesh: tiles: 8 (over z, core), rows: 16 (over y, x).
Axes of the slice: x: 4, y: 4, z: 4, core: 2. Of those that a mesh axis runs over, the one named last changes fastest.
Arguments:
- tile_values: bfloat16 [128, 8, 1024, 1024], P(('tiles', 'rows')), may hold values from -6 to 6
- tile_coords: int32 [128, 8, 4], P(('tiles', 'rows')), may hold values from 0 to 191, as said below
- tile_count: int32 [128], P(('tiles', 'rows')), may hold values from 4 to 8, as said below
- factors: float32 [4, 6144, 256], P(None, 'rows'), may hold values from -3 to 3
Outputs:
- updated: float32 [4, 6144, 256], P(None, 'rows')
The draws below stay inside these ranges and needn't reach their ends.
Inputs may be any that keep to these rules, and one draw needn't show every extreme that they name: `tile_coords`: over the live slots of one device, the four modes together name blocks of one row owner (block index // 12) at most 4 times; on every device some owner is named exactly 4 times. The same block may appear in several tiles. Slot 0 is always live. Slots from tile_count[d] on are ignored; some device has all slots live.
All inputs are finite; a program needn't handle non-finite values.
Results may differ from the reference program's by a relative error of at most 0.0033.
Values may be sent and summed in bfloat16 or wider, within the bound.
No kernel may reach another device: no remote copies, remote signals or barrier semaphores. Data moves between devices by JAX's collectives and lax.ppermute only.
A program may use at most 128 MiB of HBM per device.

```python
import jax
import jax.numpy as jnp
from jax import lax

TILE = 32
RANK = 256
SLOTS = 8
CAP = 4
BLK_DEV = 12
NB = 6144
N_ROWS = 16
DEVICES = 128


def draw_tile_coords(key, part):
    key = jax.random.fold_in(key, 11)

    def one_device(device_key):
        key_owner, key_order, key_local = jax.random.split(device_key, 3)
        owners = jnp.repeat(jnp.arange(N_ROWS, dtype=jnp.int32), CAP)
        chosen = jax.random.randint(key_owner, (), 0, N_ROWS, dtype=jnp.int32)
        scores = jax.random.permutation(key_order, N_ROWS * CAP).astype(jnp.int32)
        scores = jnp.where(owners == chosen, scores - 2 * N_ROWS * CAP, scores)
        ordering = jnp.argsort(scores, stable=True)
        picked = owners[ordering][:SLOTS * 4].reshape(SLOTS, 4)
        local_part = jax.random.randint(key_local, (SLOTS, 4), 0, BLK_DEV, dtype=jnp.int32)
        return (picked * BLK_DEV + local_part).astype(jnp.int32)
    return jax.vmap(one_device)(jax.random.split(key, DEVICES))


def draw_tile_count(key, part):
    key = jax.random.fold_in(key, 23)
    key_count, key_full = jax.random.split(key)
    counts = jax.random.randint(key_count, (DEVICES,), 4, SLOTS + 1, dtype=jnp.int32)
    fullest = jax.random.randint(key_full, (), 0, DEVICES, dtype=jnp.int32)
    return counts.at[fullest].set(SLOTS).astype(jnp.int32)


def levels(stream_key, extent, cuts, smallest, high):
    gain = 1.0
    for axis_at, blocks in cuts:
        steps = jax.random.uniform(jax.random.fold_in(jax.random.fold_in(stream_key, 6), axis_at), (blocks,), jnp.float32, smallest / len(cuts), high / len(cuts))
        gain = gain * jnp.repeat(jnp.exp(steps), extent[axis_at] // blocks).reshape((-1,) + (1,) * (len(extent) - 1 - axis_at))
    return gain


def gaussian(stream_key, extent, spread, bound, shards=(), kind=jnp.bfloat16):
    gain = levels(stream_key, extent, shards, -0.22, 0.18) if shards else 1.0
    values = jax.random.normal(stream_key, extent, jnp.float32) * spread * gain
    return jnp.minimum(jnp.maximum(values, -bound), bound).astype(kind)


def setup_inputs(seed: int = 0) -> dict:
    splits = jax.random.split(jax.random.key(seed), 5)
    tile_values = gaussian(splits[0], (DEVICES, SLOTS, TILE * TILE, TILE * TILE), 1.0, 6.0, ((0, 128),))
    tile_coords = draw_tile_coords(jax.random.fold_in(splits[4], 71), 0)
    tile_count = draw_tile_count(jax.random.fold_in(splits[4], 71), 0)
    factors = gaussian(splits[3], (4, NB, RANK), 0.5, 3.0, ((1, 16),), jnp.float32)
    return dict(tile_values=tile_values, tile_coords=tile_coords, tile_count=tile_count, factors=factors)


step_size = 0.02


def rounded(array):
    return lax.optimization_barrier(array.astype(jnp.bfloat16)).astype(jnp.float32)


def tile_gradient(tile_block, blocks):
    mode_one, mode_two, mode_three, mode_four = blocks[0], blocks[1], blocks[2], blocks[3]
    tile_edge = mode_one.shape[0]
    pair_ab = rounded((mode_one[:, None, :] * mode_two[None, :, :]).reshape(tile_edge * tile_edge, RANK))
    pair_cd = rounded((mode_three[:, None, :] * mode_four[None, :, :]).reshape(tile_edge * tile_edge, RANK))
    model_values = jnp.dot(pair_ab, pair_cd.T, precision=lax.Precision.HIGHEST)
    misfit = rounded(jnp.clip(model_values - tile_block, -1.0, 1.0))
    left_terms = jnp.dot(misfit, pair_cd, precision=lax.Precision.HIGHEST).reshape(tile_edge, tile_edge, RANK)
    right_terms = jnp.dot(misfit.T, pair_ab, precision=lax.Precision.HIGHEST).reshape(tile_edge, tile_edge, RANK)
    grad_one = jnp.sum(left_terms * mode_two[None, :, :], axis=1)
    grad_two = jnp.sum(left_terms * mode_one[:, None, :], axis=0)
    grad_three = jnp.sum(right_terms * mode_four[None, :, :], axis=1)
    grad_four = jnp.sum(right_terms * mode_three[:, None, :], axis=0)
    return jnp.stack([grad_one, grad_two, grad_three, grad_four])


def reference(tile_values, tile_coords, tile_count, factors):
    narrow = rounded(factors)
    tile_rows = tile_values.reshape(DEVICES * SLOTS, TILE * TILE, TILE * TILE)
    coord_rows = tile_coords.reshape(DEVICES * SLOTS, 4)
    alive = (jnp.arange(SLOTS)[None, :] < tile_count[:, None]).reshape(DEVICES * SLOTS)
    zero_index = jnp.zeros((), jnp.int32)

    def visit(running, scan_item):
        tile_block, coord_row, alive_flag = scan_item
        starts = [(coord_row[mode] * TILE).astype(jnp.int32) for mode in range(4)]
        blocks = jnp.stack([lax.dynamic_slice_in_dim(narrow[mode], starts[mode], TILE, 0) for mode in range(4)])

        def compute():
            return tile_gradient(tile_block.astype(jnp.float32), blocks)

        def skipped():
            return jnp.zeros((4, TILE, RANK), jnp.float32)

        gradient = lax.cond(alive_flag, compute, skipped)
        for mode in range(4):
            anchor = (zero_index + mode, starts[mode], zero_index)
            current = lax.dynamic_slice(running, anchor, (1, TILE, RANK))
            running = lax.dynamic_update_slice(running, current + gradient[mode][None], anchor)
        return running, None

    running, unused = lax.scan(visit, jnp.zeros(factors.shape, jnp.float32), (tile_rows, coord_rows, alive))
    return factors - step_size * running
```

```python
import functools

import jax
import jax.numpy as jnp
from jax import lax
from jax.experimental import pallas as pl
from jax.experimental.pallas import tpu as pltpu
from jax.sharding import PartitionSpec as P

TILE = 32
CAP = 4
EDGE = TILE * TILE
LANES = 128

step_size = 0.02

VMEM = pl.BlockSpec(memory_space=pltpu.VMEM)
SMEM = pl.BlockSpec(memory_space=pltpu.SMEM)


def request_kernel(owners, blk_dev, coords, count, wanted, slots, used):
    lines = (owners, LANES)
    row = lax.broadcasted_iota(jnp.int32, lines, 0)
    lane = lax.broadcasted_iota(jnp.int32, lines, 1)
    for owner in range(owners):
        used[owner] = 0

    def tile(slot, table):
        for mode in range(4):
            block = coords[mode, slot]
            owner = block // blk_dev
            rank = used[owner]
            used[owner] = rank + 1
            slots[slot * 4 + mode] = owner * CAP + rank
            local = mode * blk_dev + block - owner * blk_dev
            table = jnp.where((row == owner) & (lane == rank), local, table)
        return table

    table = lax.fori_loop(0, count[0], tile, jnp.full(lines, -1, jnp.int32))
    for owner in range(owners):
        wanted[owner] = jnp.broadcast_to(table[owner : owner + 1], wanted.shape[1:])


def serve_kernel(peers, asked, factors, sent, table):
    lane = lax.broadcasted_iota(jnp.int32, table.shape, 1)
    listed = jnp.full(table.shape, -1, jnp.int32)
    for peer in range(peers):
        for rank in range(CAP):
            local = asked[peer, 0, rank]
            listed = jnp.where(lane == peer * CAP + rank, local, listed)
            sent[peer, rank * TILE : (rank + 1) * TILE, :] = factors[jnp.maximum(local, 0)].astype(
                jnp.bfloat16
            )
    table[...] = listed


def tile_kernel(
    owners, parts, chunk, count, slots, blocks, tiles, out, values, misfit, pair_ab, pair_cd, grads, sem
):
    live = count[0]
    f32, bf16 = jnp.float32, jnp.bfloat16
    rank = blocks.shape[-1]

    def fetch(slot):
        place = lax.rem(slot, 2)
        return pltpu.make_async_copy(tiles.at[slot], values.at[place], sem.at[place])

    fetch(0).start()
    grads[...] = jnp.zeros_like(grads)

    def tile(slot, carry):
        @pl.when(slot + 1 < live)
        def _():
            fetch(slot + 1).start()

        names = [slots[slot * 4 + mode] for mode in range(4)]
        one, two, three, four = [
            blocks[pl.ds(pl.multiple_of(name * TILE, TILE), TILE), :].astype(f32) for name in names
        ]
        for i in range(TILE):
            at = slice(i * TILE, (i + 1) * TILE)
            pair_ab[at, :] = (one[i : i + 1] * two).astype(bf16)
            pair_cd[at, :] = (three[i : i + 1] * four).astype(bf16)
        fetch(slot).wait()
        place = lax.rem(slot, 2)
        outer = chunk // TILE
        grad_one, grad_two = [], jnp.zeros((TILE, rank), f32)
        for at in range(0, EDGE, chunk):
            model = lax.dot_general(
                pair_ab[at : at + chunk, :],
                pair_cd[...],
                (((1,), (1,)), ((), ())),
                preferred_element_type=f32,
            )
            off = jnp.clip(model - values[place, at : at + chunk, :].astype(f32), -1.0, 1.0).astype(bf16)
            misfit[at : at + chunk, :] = off
            left = jnp.dot(off, pair_cd[...], preferred_element_type=f32).reshape(outer, TILE, rank)
            grad_one.append(jnp.sum(left * two[None], axis=1))
            for i in range(outer):
                first = at // TILE + i
                grad_two = grad_two + left[i] * one[first : first + 1]
        grad_three, grad_four = [], jnp.zeros((TILE, rank), f32)
        for at in range(0, EDGE, chunk):
            right = lax.dot_general(
                misfit[:, at : at + chunk],
                pair_ab[...],
                (((0,), (0,)), ((), ())),
                preferred_element_type=f32,
            ).reshape(outer, TILE, rank)
            grad_three.append(jnp.sum(right * four[None], axis=1))
            for k in range(outer):
                first = at // TILE + k
                grad_four = grad_four + right[k] * three[first : first + 1]
        grads[names[0]] = jnp.concatenate(grad_one, 0)
        grads[names[1]] = grad_two
        grads[names[2]] = jnp.concatenate(grad_three, 0)
        grads[names[3]] = grad_four
        return carry

    lax.fori_loop(0, live, tile, 0)
    height = TILE // parts
    for owner in range(owners):
        for part in range(parts):
            out[part * owners + owner] = jnp.concatenate(
                [
                    grads[owner * CAP + place, part * height : (part + 1) * height, :]
                    for place in range(CAP)
                ],
                0,
            ).astype(bf16)


def add_kernel(peers, layer, table_0, table_1, table_2, table_3, came, total, *sums):
    tables = (table_0, table_1, table_2, table_3)
    height = total.shape[0] // sums[0].shape[0]
    for acc in sums:
        acc[...] = jnp.zeros_like(acc)
    for back, table in enumerate(tables):
        source = lax.rem(layer[0] + len(tables) - back, len(tables))

        def peer_step(peer, carry, table=table, source=source):
            message = came[source * peers + peer].astype(jnp.float32)
            for rank, acc in enumerate(sums):
                local = jnp.maximum(table[0, peer * CAP + rank], 0)
                acc[local] += message[rank * height : (rank + 1) * height]
            return carry

        lax.fori_loop(0, peers, peer_step, 0, unroll=4)
    summed = sums[0][...] + sums[1][...] + sums[2][...] + sums[3][...]
    total[...] = summed.reshape(total.shape).astype(total.dtype)


def update_kernel(layer, factors, *refs):
    own, other, out = refs[:4], refs[4:8], refs[8]
    parts = len(own)
    height = TILE // parts
    for back in range(parts):
        source = lax.rem(layer[0] + parts - back, parts)
        at = pl.ds(pl.multiple_of(source * height, height), height)
        gradient = own[back][...].astype(jnp.float32) + other[back][...].astype(jnp.float32)
        gradient = gradient.reshape(out.shape[0], height, -1)
        out[:, at, :] = factors[:, at, :] - step_size * gradient


def on_device(layers, owners, tile_values, tile_coords, tile_count, factors):
    blk_dev = factors.shape[1] // TILE
    rank = factors.shape[2]
    held = 4 * blk_dev
    slot_total = tile_values.shape[1]
    factor_blocks = factors.reshape(held, TILE, rank)
    layer = (lax.axis_index("tiles") // 2).astype(jnp.int32).reshape(1)
    bf16, f32, i32 = jnp.bfloat16, jnp.float32, jnp.int32

    wanted, slots = pl.pallas_call(
        functools.partial(request_kernel, owners, blk_dev),
        out_shape=(
            jax.ShapeDtypeStruct((owners, 8, LANES), i32),
            jax.ShapeDtypeStruct((slot_total * 4,), i32),
        ),
        in_specs=[SMEM, SMEM],
        out_specs=(VMEM, SMEM),
        scratch_shapes=[pltpu.SMEM((owners,), i32)],
        name="requests",
    )(tile_coords[0].T, tile_count)
    asked = lax.all_to_all(wanted, "rows", 0, 0)

    sent, table = pl.pallas_call(
        functools.partial(serve_kernel, owners),
        out_shape=(
            jax.ShapeDtypeStruct((owners, CAP * TILE, rank), bf16),
            jax.ShapeDtypeStruct((8, LANES), i32),
        ),
        in_specs=[SMEM, VMEM],
        out_specs=(VMEM, VMEM),
        name="serve",
    )(asked, factor_blocks)
    blocks = lax.all_to_all(sent, "rows", 0, 0).reshape(owners * CAP * TILE, rank)

    def round_trip(back):
        size = 2 * layers
        return [(i, (i + 2 * back) % size) for i in range(size)]

    tables = [table] + [lax.ppermute(table, "tiles", round_trip(back)) for back in range(1, layers)]

    flops = 3 * 2 * EDGE * EDGE * rank * slot_total
    messages = pl.pallas_call(
        functools.partial(tile_kernel, owners, layers, 256),
        out_shape=jax.ShapeDtypeStruct((layers * owners, CAP * TILE // layers, rank), bf16),
        in_specs=[SMEM, SMEM, VMEM, pl.BlockSpec(memory_space=pl.ANY)],
        out_specs=VMEM,
        scratch_shapes=[
            pltpu.VMEM((2, EDGE, EDGE), bf16),
            pltpu.VMEM((EDGE, EDGE), bf16),
            pltpu.VMEM((EDGE, rank), bf16),
            pltpu.VMEM((EDGE, rank), bf16),
            pltpu.VMEM((owners * CAP, TILE, rank), f32),
            pltpu.SemaphoreType.DMA((2,)),
        ],
        compiler_params=pltpu.CompilerParams(vmem_limit_bytes=40 << 20),
        cost_estimate=pl.CostEstimate(
            flops=flops, bytes_accessed=2 * EDGE * EDGE * slot_total, transcendentals=0
        ),
        name="tiles",
    )(tile_count, slots, blocks, tile_values[0])

    same_core = [
        [t * owners + r for t in range(core, 2 * layers, 2) for r in range(owners)] for core in range(2)
    ]
    came = lax.all_to_all(messages, ("tiles", "rows"), 0, 0, axis_index_groups=same_core)

    height = TILE // layers
    partial = pl.pallas_call(
        functools.partial(add_kernel, owners),
        out_shape=jax.ShapeDtypeStruct((held * height, rank), bf16),
        in_specs=[SMEM] * (1 + layers) + [VMEM],
        out_specs=VMEM,
        scratch_shapes=[pltpu.VMEM((held, height, rank), f32)] * CAP,
        name="add",
    )(layer, *tables, came)

    own = [partial] + [lax.ppermute(partial, "tiles", round_trip(back)) for back in range(1, layers)]
    pair = [(i, i ^ 1) for i in range(2 * layers)]
    other = [lax.ppermute(piece, "tiles", pair) for piece in own]

    updated = pl.pallas_call(
        update_kernel,
        out_shape=jax.ShapeDtypeStruct(factor_blocks.shape, f32),
        in_specs=[SMEM] + [VMEM] * 9,
        out_specs=VMEM,
        name="update",
    )(layer, factor_blocks, *own, *other)
    return updated.reshape(factors.shape)


def solution(mesh):
    layers, owners = mesh.shape["tiles"] // 2, mesh.shape["rows"]
    return jax.shard_map(
        functools.partial(on_device, layers, owners),
        mesh=mesh,
        in_specs=(
            P(("tiles", "rows"), None, None, None),
            P(("tiles", "rows"), None, None),
            P(("tiles", "rows")),
            P(None, "rows", None),
        ),
        out_specs=P(None, "rows", None),
        check_vma=False,
    )
```

```python
import functools

import jax
import jax.numpy as jnp
from jax import lax
from jax.experimental import pallas as pl
from jax.experimental.pallas import tpu as pltpu
from jax.sharding import PartitionSpec as P

TILE = 32
CAP = 4
EDGE = TILE * TILE
LANES = 128

step_size = 0.02

VMEM = pl.BlockSpec(memory_space=pltpu.VMEM)
SMEM = pl.BlockSpec(memory_space=pltpu.SMEM)
ANY = pl.BlockSpec(memory_space=pl.ANY)


def in_vmem(array):
    return pltpu.with_memory_space_constraint(array, pltpu.VMEM)


def request_kernel(owners, blk_dev, coords, count, wanted, slots, used):
    lines = (owners, LANES)
    row = lax.broadcasted_iota(jnp.int32, lines, 0)
    lane = lax.broadcasted_iota(jnp.int32, lines, 1)
    for owner in range(owners):
        used[owner] = 0

    def tile(slot, table):
        for mode in range(4):
            block = coords[mode, slot]
            owner = block // blk_dev
            rank = used[owner]
            used[owner] = rank + 1
            slots[slot * 4 + mode] = owner * CAP + rank
            local = mode * blk_dev + block - owner * blk_dev
            table = jnp.where((row == owner) & (lane == rank), local, table)
        return table

    table = lax.fori_loop(0, count[0], tile, jnp.full(lines, -1, jnp.int32))
    for owner in range(owners):
        wanted[owner] = jnp.broadcast_to(table[owner : owner + 1], wanted.shape[1:])


def serve_kernel(peers, asked, factors, tiles, sent, table, first, listed, held, ready, sems):
    copy = pltpu.make_async_copy(asked.at[:, 0, :], listed, sems.at[0])
    copy.start()
    whole = pltpu.make_async_copy(factors, held, sems.at[6])
    whole.start()
    early = pltpu.make_async_copy(tiles.at[0], first, sems.at[1])
    early.start()
    copy.wait()
    lane = lax.broadcasted_iota(jnp.int32, table.shape, 1)
    line = jnp.full(table.shape, -1, jnp.int32)
    for peer in range(peers):
        for rank in range(CAP):
            line = jnp.where(lane == peer * CAP + rank, listed[peer, rank], line)
    table[...] = line
    whole.wait()
    group = peers // 4
    copies = []
    for peer in range(peers):
        for rank in range(CAP):
            local = jnp.maximum(listed[peer, rank], 0)
            ready[peer, rank * TILE : (rank + 1) * TILE, :] = held[local].astype(jnp.bfloat16)
        if peer % group == group - 1:
            some = slice(peer + 1 - group, peer + 1)
            copies.append(
                pltpu.make_async_copy(ready.at[some], sent.at[some], sems.at[2 + peer // group])
            )
            copies[-1].start()
    for copy in copies:
        copy.wait()
    early.wait()


def tile_kernel(
    owners, parts, chunk, count, slots, blocks, early, tiles, out, values, misfit, pair_ab, pair_cd, grads, sems
):
    live, total = count[0], tiles.shape[0]
    f32, bf16 = jnp.float32, jnp.bfloat16
    rank = blocks.shape[-1]
    spare = owners * CAP

    def fetch(slot):
        return pltpu.make_async_copy(tiles.at[slot], values.at[slot], sems.at[slot])

    for slot in range(1, total):
        fetch(slot).start()
    grads[...] = jnp.zeros_like(grads)

    def tile(slot, tile_at):
        names = [jnp.where(slot < live, slots[slot * 4 + mode], spare) for mode in range(4)]
        one, two, three, four = [
            blocks[pl.ds(pl.multiple_of(jnp.minimum(name, spare - 1) * TILE, TILE), TILE), :].astype(f32)
            for name in names
        ]
        for i in range(TILE):
            at = slice(i * TILE, (i + 1) * TILE)
            pair_ab[at, :] = (one[i : i + 1] * two).astype(bf16)
            pair_cd[at, :] = (three[i : i + 1] * four).astype(bf16)
        outer = chunk // TILE
        grad_one, grad_two = [], jnp.zeros((TILE, rank), f32)
        for at in range(0, EDGE, chunk):
            model = lax.dot_general(
                pair_ab[at : at + chunk, :],
                pair_cd[...],
                (((1,), (1,)), ((), ())),
                preferred_element_type=f32,
            )
            off = (model - tile_at[at : at + chunk, :].astype(f32)).astype(bf16)
            off = jnp.clip(off, jnp.asarray(-1.0, bf16), jnp.asarray(1.0, bf16))
            misfit[at : at + chunk, :] = off
            left = jnp.dot(off, pair_cd[...], preferred_element_type=f32).reshape(outer, TILE, rank)
            grad_one.append(jnp.sum(left * two[None], axis=1))
            for i in range(outer):
                first = at // TILE + i
                grad_two = grad_two + left[i] * one[first : first + 1]
        grad_three, grad_four = [], jnp.zeros((TILE, rank), f32)
        for at in range(0, EDGE, chunk):
            right = lax.dot_general(
                misfit[:, at : at + chunk],
                pair_ab[...],
                (((0,), (0,)), ((), ())),
                preferred_element_type=f32,
            ).reshape(outer, TILE, rank)
            grad_three.append(jnp.sum(right * four[None], axis=1))
            for k in range(outer):
                first = at // TILE + k
                grad_four = grad_four + right[k] * three[first : first + 1]
        grads[names[0]] = jnp.concatenate(grad_one, 0)
        grads[names[1]] = grad_two
        grads[names[2]] = jnp.concatenate(grad_three, 0)
        grads[names[3]] = grad_four

    def later(slot, carry):
        fetch(slot).wait()
        tile(slot, values.at[slot])
        return carry

    tile(0, early)
    lax.fori_loop(1, total, later, 0)
    height = TILE // parts
    for owner in range(owners):
        for part in range(parts):
            out[part * owners + owner] = jnp.concatenate(
                [
                    grads[owner * CAP + place, part * height : (part + 1) * height, :]
                    for place in range(CAP)
                ],
                0,
            ).astype(bf16)


def add_kernel(peers, layer, table_0, table_1, table_2, table_3, came, total, *sums):
    tables = (table_0, table_1, table_2, table_3)
    height = total.shape[0] // sums[0].shape[0]
    for acc in sums:
        acc[...] = jnp.zeros_like(acc)
    for back, table in enumerate(tables):
        source = lax.rem(layer[0] + len(tables) - back, len(tables))

        def peer_step(peer, carry, table=table, source=source):
            message = came[source * peers + peer].astype(jnp.float32)
            for rank, acc in enumerate(sums):
                local = jnp.maximum(table[0, peer * CAP + rank], 0)
                acc[local] += message[rank * height : (rank + 1) * height]
            return carry

        lax.fori_loop(0, peers, peer_step, 0, unroll=4)
    summed = sums[0][...] + sums[1][...] + sums[2][...] + sums[3][...]
    total[...] = summed.reshape(total.shape).astype(total.dtype)


def update_kernel(layer, factors, *refs):
    own, other, (out, before, stepped, sems) = refs[:4], refs[4:8], refs[8:]
    parts = len(own)
    height = TILE // parts
    held = factors.shape[0] // 4
    modes = [slice(mode * held, (mode + 1) * held) for mode in range(4)]
    brought = [
        pltpu.make_async_copy(factors.at[blocks], before.at[blocks], sems.at[mode])
        for mode, blocks in enumerate(modes)
    ]
    stored = [
        pltpu.make_async_copy(stepped.at[blocks], out.at[blocks], sems.at[4 + mode])
        for mode, blocks in enumerate(modes)
    ]
    for copy in brought:
        copy.start()
    for mode, blocks in enumerate(modes):
        brought[mode].wait()
        lines = slice(mode * held * height, (mode + 1) * held * height)
        for back in range(parts):
            source = lax.rem(layer[0] + parts - back, parts)
            at = pl.ds(pl.multiple_of(source * height, height), height)
            gradient = own[back][lines, :].astype(jnp.float32) + other[back][lines, :].astype(jnp.float32)
            gradient = gradient.reshape(held, height, -1)
            stepped[blocks, at, :] = before[blocks, at, :] - step_size * gradient
        stored[mode].start()
    for copy in stored:
        copy.wait()


def on_device(layers, owners, tile_values, tile_coords, tile_count, factors):
    blk_dev = factors.shape[1] // TILE
    rank = factors.shape[2]
    held = 4 * blk_dev
    slot_total = tile_values.shape[1]
    factor_blocks = factors.reshape(held, TILE, rank)
    layer = (lax.axis_index("tiles") // 2).astype(jnp.int32).reshape(1)
    bf16, f32, i32 = jnp.bfloat16, jnp.float32, jnp.int32

    wanted, slots = pl.pallas_call(
        functools.partial(request_kernel, owners, blk_dev),
        out_shape=(
            pltpu.VMEM((owners, 8, LANES), i32),
            jax.ShapeDtypeStruct((slot_total * 4,), i32),
        ),
        in_specs=[SMEM, SMEM],
        out_specs=(VMEM, SMEM),
        scratch_shapes=[pltpu.SMEM((owners,), i32)],
        name="requests",
    )(tile_coords[0].T, tile_count)
    asked = lax.all_to_all(wanted, "rows", 0, 0)

    sent, table, first = pl.pallas_call(
        functools.partial(serve_kernel, owners),
        out_shape=(
            jax.ShapeDtypeStruct((owners, CAP * TILE, rank), bf16),
            jax.ShapeDtypeStruct((8, LANES), i32),
            pltpu.VMEM(tile_values.shape[2:], bf16),
        ),
        in_specs=[ANY, ANY, ANY],
        out_specs=(ANY, VMEM, VMEM),
        scratch_shapes=[
            pltpu.SMEM((owners, LANES), i32),
            pltpu.VMEM(factor_blocks.shape, f32),
            pltpu.VMEM((owners, CAP * TILE, rank), bf16),
            pltpu.SemaphoreType.DMA((7,)),
        ],
        name="serve",
    )(in_vmem(asked), factor_blocks, tile_values[0])
    blocks = lax.all_to_all(sent, "rows", 0, 0).reshape(owners * CAP * TILE, rank)

    def round_trip(back):
        size = 2 * layers
        return [(i, (i + 2 * back) % size) for i in range(size)]

    tables = [table] + [lax.ppermute(table, "tiles", round_trip(back)) for back in range(1, layers)]

    slots, tables, layer = lax.optimization_barrier((slots, tables, layer))
    flops = 3 * 2 * EDGE * EDGE * rank * slot_total
    messages = pl.pallas_call(
        functools.partial(tile_kernel, owners, layers, 256),
        out_shape=pltpu.VMEM((layers * owners, CAP * TILE // layers, rank), bf16),
        in_specs=[SMEM, SMEM, VMEM, VMEM, ANY],
        out_specs=VMEM,
        scratch_shapes=[
            pltpu.VMEM((slot_total, EDGE, EDGE), bf16),
            pltpu.VMEM((EDGE, EDGE), bf16),
            pltpu.VMEM((EDGE, rank), bf16),
            pltpu.VMEM((EDGE, rank), bf16),
            pltpu.VMEM((owners * CAP + 1, TILE, rank), f32),
            pltpu.SemaphoreType.DMA((slot_total,)),
        ],
        compiler_params=pltpu.CompilerParams(vmem_limit_bytes=40 << 20),
        cost_estimate=pl.CostEstimate(
            flops=flops, bytes_accessed=2 * EDGE * EDGE * slot_total, transcendentals=0
        ),
        name="tiles",
    )(tile_count, slots, in_vmem(blocks), in_vmem(first), tile_values[0])

    same_core = [
        [t * owners + r for t in range(core, 2 * layers, 2) for r in range(owners)] for core in range(2)
    ]
    came = lax.all_to_all(messages, ("tiles", "rows"), 0, 0, axis_index_groups=same_core)

    height = TILE // layers
    partial = pl.pallas_call(
        functools.partial(add_kernel, owners),
        out_shape=pltpu.VMEM((held * height, rank), bf16),
        in_specs=[SMEM] * (1 + layers) + [VMEM],
        out_specs=VMEM,
        scratch_shapes=[pltpu.VMEM((held, height, rank), f32)] * CAP,
        name="add",
    )(layer, *tables, in_vmem(came))

    own = [partial] + [lax.ppermute(partial, "tiles", round_trip(back)) for back in range(1, layers)]
    pair = [(i, i ^ 1) for i in range(2 * layers)]
    other = [lax.ppermute(piece, "tiles", pair) for piece in own]

    updated = pl.pallas_call(
        update_kernel,
        out_shape=jax.ShapeDtypeStruct(factor_blocks.shape, f32),
        in_specs=[SMEM, ANY] + [VMEM] * 8,
        out_specs=ANY,
        scratch_shapes=[pltpu.VMEM(factor_blocks.shape, f32)] * 2 + [pltpu.SemaphoreType.DMA((8,))],
        name="update",
    )(layer, factor_blocks, *[in_vmem(piece) for piece in own + other])
    return updated.reshape(factors.shape)


def solution(mesh):
    layers, owners = mesh.shape["tiles"] // 2, mesh.shape["rows"]
    return jax.shard_map(
        functools.partial(on_device, layers, owners),
        mesh=mesh,
        in_specs=(
            P(("tiles", "rows"), None, None, None),
            P(("tiles", "rows"), None, None),
            P(("tiles", "rows")),
            P(None, "rows", None),
        ),
        out_specs=P(None, "rows", None),
        check_vma=False,
    )
```

```python
import functools

import jax
import jax.numpy as jnp
from jax import lax
from jax.experimental import pallas as pl
from jax.experimental.pallas import tpu as pltpu
from jax.sharding import PartitionSpec as P

TILE = 32
CAP = 4
EDGE = TILE * TILE
LANES = 128

step_size = 0.02

VMEM = pl.BlockSpec(memory_space=pltpu.VMEM)
SMEM = pl.BlockSpec(memory_space=pltpu.SMEM)
ANY = pl.BlockSpec(memory_space=pl.ANY)
HBM = pl.BlockSpec(memory_space=pltpu.HBM)


def in_hbm(array):
    return pltpu.with_memory_space_constraint(array, pltpu.HBM)


def in_vmem(array):
    return pltpu.with_memory_space_constraint(array, pltpu.VMEM)


def request_kernel(owners, blk_dev, coords, count, wanted, slots, used):
    lines = (owners, LANES)
    row = lax.broadcasted_iota(jnp.int32, lines, 0)
    lane = lax.broadcasted_iota(jnp.int32, lines, 1)
    for owner in range(owners):
        used[owner] = 0

    def tile(slot, table):
        for mode in range(4):
            block = coords[mode, slot]
            owner = block // blk_dev
            rank = used[owner]
            used[owner] = rank + 1
            slots[slot * 4 + mode] = owner * CAP + rank
            local = mode * blk_dev + block - owner * blk_dev
            table = jnp.where((row == owner) & (lane == rank), local, table)
        return table

    table = lax.fori_loop(0, count[0], tile, jnp.full(lines, -1, jnp.int32))
    for owner in range(owners):
        wanted[owner] = jnp.broadcast_to(table[owner : owner + 1], wanted.shape[1:])


def prepare_kernel(factors, tiles, narrow, first, wide, sems):
    whole = pltpu.make_async_copy(factors, wide, sems.at[0])
    early = pltpu.make_async_copy(tiles.at[0], first, sems.at[1])
    whole.start()
    early.start()
    whole.wait()
    narrow[...] = wide[...].astype(narrow.dtype)
    early.wait()


def bring_kernel(ready, factors, kept, sem):
    del ready
    copy = pltpu.make_async_copy(factors, kept, sem)
    copy.start()
    copy.wait()


def serve_kernel(peers, asked, narrow, sent, table, listed, ready, sems):
    copy = pltpu.make_async_copy(asked.at[:, 0, :], listed, sems.at[0])
    copy.start()
    copy.wait()
    lane = lax.broadcasted_iota(jnp.int32, table.shape, 1)
    line = jnp.full(table.shape, -1, jnp.int32)
    group = peers // 4
    copies = []
    for peer in range(peers):
        for rank in range(CAP):
            local = listed[peer, rank]
            line = jnp.where(lane == peer * CAP + rank, local, line)
            ready[peer, rank * TILE : (rank + 1) * TILE, :] = narrow[jnp.maximum(local, 0)]
        if peer % group == group - 1:
            some = slice(peer + 1 - group, peer + 1)
            copies.append(
                pltpu.make_async_copy(ready.at[some], sent.at[some], sems.at[1 + peer // group])
            )
            copies[-1].start()
    table[...] = line
    for copy in copies:
        copy.wait()


def tile_kernel(
    owners, parts, chunk, count, slots, blocks, early, tiles, out, values, misfit, pair_ab, pair_cd, grads, sems
):
    live, total = count[0], tiles.shape[0]
    f32, bf16 = jnp.float32, jnp.bfloat16
    rank = blocks.shape[-1]
    spare = owners * CAP

    def fetch(slot):
        return pltpu.make_async_copy(tiles.at[slot], values.at[slot], sems.at[slot])

    for slot in range(1, total):
        fetch(slot).start()
    grads[...] = jnp.zeros_like(grads)

    def tile(slot, tile_at):
        names = [jnp.where(slot < live, slots[slot * 4 + mode], spare) for mode in range(4)]
        one, two, three, four = [
            blocks[pl.ds(pl.multiple_of(jnp.minimum(name, spare - 1) * TILE, TILE), TILE), :].astype(f32)
            for name in names
        ]
        for i in range(TILE):
            at = slice(i * TILE, (i + 1) * TILE)
            pair_ab[at, :] = (one[i : i + 1] * two).astype(bf16)
            pair_cd[at, :] = (three[i : i + 1] * four).astype(bf16)
        def spread(terms, first, other, kept):
            terms = terms.reshape(-1, TILE, rank)
            for i in range(terms.shape[0]):
                kept = kept + terms[i] * first[i : i + 1]
            return jnp.sum(terms * other[None], axis=1), kept

        def left_of(at, kept):
            left = jnp.dot(misfit[at : at + 2 * chunk, :], pair_cd[...], preferred_element_type=f32)
            return spread(left, one[at // TILE : (at + 2 * chunk) // TILE], two, kept)

        grad_one, grad_two = [], jnp.zeros((TILE, rank), f32)
        for at in range(0, EDGE, 2 * chunk):
            lines = slice(at, at + 2 * chunk)
            model = lax.dot_general(
                pair_ab[lines, :], pair_cd[...], (((1,), (1,)), ((), ())), preferred_element_type=f32
            )
            off = (model - tile_at[lines, :].astype(f32)).astype(bf16)
            misfit[lines, :] = jnp.clip(off, jnp.asarray(-1.0, bf16), jnp.asarray(1.0, bf16))
            if at:
                part_one, grad_two = left_of(at - 2 * chunk, grad_two)
                grad_one.append(part_one)
        part_one, grad_two = left_of(EDGE - 2 * chunk, grad_two)
        grad_one.append(part_one)
        grad_three, grad_four = [], jnp.zeros((TILE, rank), f32)
        for at in range(0, EDGE, chunk):
            right = lax.dot_general(
                misfit[:, at : at + chunk],
                pair_ab[...],
                (((0,), (0,)), ((), ())),
                preferred_element_type=f32,
            )
            first = three[at // TILE : (at + chunk) // TILE]
            part_three, grad_four = spread(right, first, four, grad_four)
            grad_three.append(part_three)
        grads[names[0]] = jnp.concatenate(grad_one, 0)
        grads[names[1]] = grad_two
        grads[names[2]] = jnp.concatenate(grad_three, 0)
        grads[names[3]] = grad_four

    def later(slot, carry):
        fetch(slot).wait()
        tile(slot, values.at[slot])
        return carry

    tile(0, early)
    lax.fori_loop(1, total, later, 0)
    height = TILE // parts
    for owner in range(owners):
        for part in range(parts):
            out[part * owners + owner] = jnp.concatenate(
                [
                    grads[owner * CAP + place, part * height : (part + 1) * height, :]
                    for place in range(CAP)
                ],
                0,
            ).astype(bf16)


def add_kernel(peers, layer, table_0, table_1, table_2, table_3, came, total, *sums):
    tables = (table_0, table_1, table_2, table_3)
    height = total.shape[0] // sums[0].shape[0]
    for acc in sums:
        acc[...] = jnp.zeros_like(acc)
    for back, table in enumerate(tables):
        source = lax.rem(layer[0] + len(tables) - back, len(tables))

        def peer_step(peer, carry, table=table, source=source):
            message = came[source * peers + peer].astype(jnp.float32)
            for rank, acc in enumerate(sums):
                local = jnp.maximum(table[0, peer * CAP + rank], 0)
                acc[local] += message[rank * height : (rank + 1) * height]
            return carry

        lax.fori_loop(0, peers, peer_step, 0, unroll=4)
    summed = sums[0][...] + sums[1][...] + sums[2][...] + sums[3][...]
    total[...] = summed.reshape(total.shape).astype(total.dtype)


def update_kernel(layer, factors, *refs):
    own, other, (out, stepped, sems) = refs[:4], refs[4:8], refs[8:]
    parts = len(own)
    height = TILE // parts
    held = factors.shape[0] // 4
    copies = []
    for mode in range(4):
        blocks = slice(mode * held, (mode + 1) * held)
        lines = slice(mode * held * height, (mode + 1) * held * height)
        for back in range(parts):
            source = lax.rem(layer[0] + parts - back, parts)
            at = pl.ds(pl.multiple_of(source * height, height), height)
            gradient = own[back][lines, :].astype(jnp.float32) + other[back][lines, :].astype(jnp.float32)
            gradient = gradient.reshape(held, height, -1)
            stepped[blocks, at, :] = factors[blocks, at, :] - step_size * gradient
        copies.append(pltpu.make_async_copy(stepped.at[blocks], out.at[blocks], sems.at[mode]))
        copies[-1].start()
    for copy in copies:
        copy.wait()


def on_device(layers, owners, tile_values, tile_coords, tile_count, factors):
    blk_dev = factors.shape[1] // TILE
    rank = factors.shape[2]
    held = 4 * blk_dev
    slot_total = tile_values.shape[1]
    factor_blocks = factors.reshape(held, TILE, rank)
    layer = (lax.axis_index("tiles") // 2).astype(jnp.int32).reshape(1)
    bf16, f32, i32 = jnp.bfloat16, jnp.float32, jnp.int32

    small = pltpu.CompilerParams(vmem_limit_bytes=8 << 20)
    wanted, slots = pl.pallas_call(
        functools.partial(request_kernel, owners, blk_dev),
        out_shape=(
            pltpu.VMEM((owners, 8, LANES), i32),
            jax.ShapeDtypeStruct((slot_total * 4,), i32),
        ),
        in_specs=[SMEM, SMEM],
        out_specs=(VMEM, SMEM),
        scratch_shapes=[pltpu.SMEM((owners,), i32)],
        name="requests",
    )(tile_coords[0].T, tile_count)
    asked = lax.all_to_all(wanted, "rows", 0, 0)

    narrow, first = pl.pallas_call(
        prepare_kernel,
        out_shape=(pltpu.VMEM(factor_blocks.shape, bf16), pltpu.VMEM(tile_values.shape[2:], bf16)),
        in_specs=[HBM, HBM],
        out_specs=(VMEM, VMEM),
        scratch_shapes=[pltpu.VMEM(factor_blocks.shape, f32), pltpu.SemaphoreType.DMA((2,))],
        compiler_params=small,
        cost_estimate=pl.CostEstimate(flops=0, bytes_accessed=4 << 20, transcendentals=0),
        name="prepare",
    )(in_hbm(factor_blocks), in_hbm(tile_values[0]))
    sent, table = pl.pallas_call(
        functools.partial(serve_kernel, owners),
        out_shape=(
            jax.ShapeDtypeStruct((owners, CAP * TILE, rank), bf16),
            jax.ShapeDtypeStruct((8, LANES), i32),
        ),
        in_specs=[ANY, VMEM],
        out_specs=(ANY, VMEM),
        scratch_shapes=[
            pltpu.SMEM((owners, LANES), i32),
            pltpu.VMEM((owners, CAP * TILE, rank), bf16),
            pltpu.SemaphoreType.DMA((5,)),
        ],
        compiler_params=small,
        name="serve",
    )(in_vmem(asked), in_vmem(narrow))
    blocks = lax.all_to_all(sent, "rows", 0, 0).reshape(owners * CAP * TILE, rank)

    def round_trip(back):
        size = 2 * layers
        return [(i, (i + 2 * back) % size) for i in range(size)]

    tables = [table] + [lax.ppermute(table, "tiles", round_trip(back)) for back in range(1, layers)]

    slots, tables, layer = lax.optimization_barrier((slots, tables, layer))
    flops = 3 * 2 * EDGE * EDGE * rank * slot_total
    messages = pl.pallas_call(
        functools.partial(tile_kernel, owners, layers, 256),
        out_shape=pltpu.VMEM((layers * owners, CAP * TILE // layers, rank), bf16),
        in_specs=[SMEM, SMEM, VMEM, VMEM, HBM],
        out_specs=VMEM,
        scratch_shapes=[
            pltpu.VMEM((slot_total, EDGE, EDGE), bf16),
            pltpu.VMEM((EDGE, EDGE), bf16),
            pltpu.VMEM((EDGE, rank), bf16),
            pltpu.VMEM((EDGE, rank), bf16),
            pltpu.VMEM((owners * CAP + 1, TILE, rank), f32),
            pltpu.SemaphoreType.DMA((slot_total,)),
        ],
        compiler_params=pltpu.CompilerParams(vmem_limit_bytes=32 << 20),
        cost_estimate=pl.CostEstimate(
            flops=flops, bytes_accessed=2 * EDGE * EDGE * slot_total, transcendentals=0
        ),
        name="tiles",
    )(tile_count, slots, in_vmem(blocks), in_vmem(first), in_hbm(tile_values[0]))

    same_core = [
        [t * owners + r for t in range(core, 2 * layers, 2) for r in range(owners)] for core in range(2)
    ]
    came = lax.all_to_all(messages, ("tiles", "rows"), 0, 0, axis_index_groups=same_core)

    height = TILE // layers
    partial = pl.pallas_call(
        functools.partial(add_kernel, owners),
        out_shape=pltpu.VMEM((held * height, rank), bf16),
        in_specs=[SMEM] * (1 + layers) + [VMEM],
        out_specs=VMEM,
        scratch_shapes=[pltpu.VMEM((held, height, rank), f32)] * CAP,
        compiler_params=small,
        name="add",
    )(layer, *tables, in_vmem(came))

    own = [partial] + [lax.ppermute(partial, "tiles", round_trip(back)) for back in range(1, layers)]
    pair = [(i, i ^ 1) for i in range(2 * layers)]
    other = [lax.ppermute(piece, "tiles", pair) for piece in own]

    kept = pl.pallas_call(
        bring_kernel,
        out_shape=pltpu.VMEM(factor_blocks.shape, f32),
        in_specs=[ANY, HBM],
        out_specs=VMEM,
        scratch_shapes=[pltpu.SemaphoreType.DMA],
        compiler_params=small,
        cost_estimate=pl.CostEstimate(flops=0, bytes_accessed=4 << 20, transcendentals=0),
        name="bring",
    )(partial, in_hbm(factor_blocks))
    updated = pl.pallas_call(
        update_kernel,
        out_shape=jax.ShapeDtypeStruct(factor_blocks.shape, f32),
        in_specs=[SMEM] + [VMEM] * 9,
        out_specs=ANY,
        scratch_shapes=[pltpu.VMEM(factor_blocks.shape, f32), pltpu.SemaphoreType.DMA((4,))],
        compiler_params=small,
        name="update",
    )(layer, in_vmem(kept), *[in_vmem(piece) for piece in own + other])
    return updated.reshape(factors.shape)


def solution(mesh):
    layers, owners = mesh.shape["tiles"] // 2, mesh.shape["rows"]
    return jax.shard_map(
        functools.partial(on_device, layers, owners),
        mesh=mesh,
        in_specs=(
            P(("tiles", "rows"), None, None, None),
            P(("tiles", "rows"), None, None),
            P(("tiles", "rows")),
            P(None, "rows", None),
        ),
        out_specs=P(None, "rows", None),
        check_vma=False,
    )
```

```python
import functools

import jax
import jax.numpy as jnp
from jax import lax
from jax.experimental import pallas as pl
from jax.experimental.pallas import tpu as pltpu
from jax.sharding import PartitionSpec as P

TILE = 32
CAP = 4
EDGE = TILE * TILE
LANES = 128

step_size = 0.02

VMEM = pl.BlockSpec(memory_space=pltpu.VMEM)
SMEM = pl.BlockSpec(memory_space=pltpu.SMEM)
ANY = pl.BlockSpec(memory_space=pl.ANY)
HBM = pl.BlockSpec(memory_space=pltpu.HBM)


def in_hbm(array):
    return pltpu.with_memory_space_constraint(array, pltpu.HBM)


def in_vmem(array):
    return pltpu.with_memory_space_constraint(array, pltpu.VMEM)


def request_kernel(owners, blk_dev, coords, count, wanted, slots, used):
    lines = (owners, LANES)
    row = lax.broadcasted_iota(jnp.int32, lines, 0)
    lane = lax.broadcasted_iota(jnp.int32, lines, 1)
    for owner in range(owners):
        used[owner] = 0

    def tile(slot, table):
        for mode in range(4):
            block = coords[mode, slot]
            owner = block // blk_dev
            rank = used[owner]
            used[owner] = rank + 1
            slots[slot * 4 + mode] = owner * CAP + rank
            local = mode * blk_dev + block - owner * blk_dev
            table = jnp.where((row == owner) & (lane == rank), local, table)
        return table

    table = lax.fori_loop(0, count[0], tile, jnp.full(lines, -1, jnp.int32))
    for owner in range(owners):
        wanted[owner] = jnp.broadcast_to(table[owner : owner + 1], wanted.shape[1:])


def prepare_kernel(factors, tiles, narrow, first, wide, sems):
    whole = pltpu.make_async_copy(factors, wide, sems.at[0])
    early = pltpu.make_async_copy(tiles.at[0], first, sems.at[1])
    whole.start()
    early.start()
    whole.wait()
    narrow[...] = wide[...].astype(narrow.dtype)
    early.wait()


def bring_kernel(ready, factors, kept, sem):
    del ready
    copy = pltpu.make_async_copy(factors, kept, sem)
    copy.start()
    copy.wait()


def serve_kernel(peers, asked, narrow, sent, table, listed, ready, sems):
    copy = pltpu.make_async_copy(asked.at[:, 0, :], listed, sems.at[0])
    copy.start()
    copy.wait()
    lane = lax.broadcasted_iota(jnp.int32, table.shape, 1)
    line = jnp.full(table.shape, -1, jnp.int32)
    group = peers // 4
    copies = []
    for peer in range(peers):
        for rank in range(CAP):
            local = listed[peer, rank]
            line = jnp.where(lane == peer * CAP + rank, local, line)
            ready[peer, rank * TILE : (rank + 1) * TILE, :] = narrow[jnp.maximum(local, 0)]
        if peer % group == group - 1:
            some = slice(peer + 1 - group, peer + 1)
            copies.append(
                pltpu.make_async_copy(ready.at[some], sent.at[some], sems.at[1 + peer // group])
            )
            copies[-1].start()
    table[...] = line
    for copy in copies:
        copy.wait()


def tile_kernel(
    owners, parts, chunk, count, slots, blocks, early, tiles, out, values, misfit, pair_ab, pair_cd, grads, sems
):
    live, total = count[0], tiles.shape[0]
    f32, bf16 = jnp.float32, jnp.bfloat16
    rank = blocks.shape[-1]

    def fetch(slot):
        return pltpu.make_async_copy(tiles.at[slot], values.at[slot], sems.at[slot])

    for slot in range(1, total):

        @pl.when(slot < live)
        def _():
            fetch(slot).start()

    grads[...] = jnp.zeros_like(grads)

    def tile(slot, tile_at):
        names = [slots[slot * 4 + mode] for mode in range(4)]
        one, two, three, four = [
            blocks[pl.ds(pl.multiple_of(name * TILE, TILE), TILE), :].astype(f32)
            for name in names
        ]
        for i in range(TILE):
            at = slice(i * TILE, (i + 1) * TILE)
            pair_ab[at, :] = (one[i : i + 1] * two).astype(bf16)
            pair_cd[at, :] = (three[i : i + 1] * four).astype(bf16)
        def spread(terms, first, other, kept):
            terms = terms.reshape(-1, TILE, rank)
            for i in range(terms.shape[0]):
                kept = kept + terms[i] * first[i : i + 1]
            return jnp.sum(terms * other[None], axis=1), kept

        def left_of(at, kept):
            left = jnp.dot(misfit[at : at + 2 * chunk, :], pair_cd[...], preferred_element_type=f32)
            return spread(left, one[at // TILE : (at + 2 * chunk) // TILE], two, kept)

        grad_one, grad_two = [], jnp.zeros((TILE, rank), f32)
        for at in range(0, EDGE, 2 * chunk):
            lines = slice(at, at + 2 * chunk)
            model = lax.dot_general(
                pair_ab[lines, :], pair_cd[...], (((1,), (1,)), ((), ())), preferred_element_type=f32
            )
            off = (model - tile_at[lines, :].astype(f32)).astype(bf16)
            misfit[lines, :] = jnp.clip(off, jnp.asarray(-1.0, bf16), jnp.asarray(1.0, bf16))
            if at:
                part_one, grad_two = left_of(at - 2 * chunk, grad_two)
                grad_one.append(part_one)
        part_one, grad_two = left_of(EDGE - 2 * chunk, grad_two)
        grad_one.append(part_one)
        grad_three, grad_four = [], jnp.zeros((TILE, rank), f32)
        for at in range(0, EDGE, chunk):
            right = lax.dot_general(
                misfit[:, at : at + chunk],
                pair_ab[...],
                (((0,), (0,)), ((), ())),
                preferred_element_type=f32,
            )
            first = three[at // TILE : (at + chunk) // TILE]
            part_three, grad_four = spread(right, first, four, grad_four)
            grad_three.append(part_three)
        grads[names[0]] = jnp.concatenate(grad_one, 0)
        grads[names[1]] = grad_two
        grads[names[2]] = jnp.concatenate(grad_three, 0)
        grads[names[3]] = grad_four

    def later(slot, carry):
        fetch(slot).wait()
        tile(slot, values.at[slot])
        return carry

    tile(0, early)
    lax.fori_loop(1, live, later, 0)
    height = TILE // parts
    for owner in range(owners):
        for part in range(parts):
            out[part * owners + owner] = jnp.concatenate(
                [
                    grads[owner * CAP + place, part * height : (part + 1) * height, :]
                    for place in range(CAP)
                ],
                0,
            ).astype(bf16)


def add_kernel(peers, layer, table_0, table_1, table_2, table_3, came, total, *sums):
    tables = (table_0, table_1, table_2, table_3)
    height = total.shape[0] // sums[0].shape[0]
    for acc in sums:
        acc[...] = jnp.zeros_like(acc)
    for back, table in enumerate(tables):
        source = lax.rem(layer[0] + len(tables) - back, len(tables))

        def peer_step(peer, carry, table=table, source=source):
            message = came[source * peers + peer].astype(jnp.float32)
            for rank, acc in enumerate(sums):
                local = jnp.maximum(table[0, peer * CAP + rank], 0)
                acc[local] += message[rank * height : (rank + 1) * height]
            return carry

        lax.fori_loop(0, peers, peer_step, 0, unroll=4)
    summed = sums[0][...] + sums[1][...] + sums[2][...] + sums[3][...]
    total[...] = summed.reshape(total.shape).astype(total.dtype)


def update_kernel(layer, factors, *refs):
    own, other, (out, stepped, sems) = refs[:4], refs[4:8], refs[8:]
    parts = len(own)
    height = TILE // parts
    held = factors.shape[0] // 4
    copies = []
    for mode in range(4):
        blocks = slice(mode * held, (mode + 1) * held)
        lines = slice(mode * held * height, (mode + 1) * held * height)
        for back in range(parts):
            source = lax.rem(layer[0] + parts - back, parts)
            at = pl.ds(pl.multiple_of(source * height, height), height)
            gradient = own[back][lines, :].astype(jnp.float32) + other[back][lines, :].astype(jnp.float32)
            gradient = gradient.reshape(held, height, -1)
            stepped[blocks, at, :] = factors[blocks, at, :] - step_size * gradient
        copies.append(pltpu.make_async_copy(stepped.at[blocks], out.at[blocks], sems.at[mode]))
        copies[-1].start()
    for copy in copies:
        copy.wait()


def on_device(layers, owners, tile_values, tile_coords, tile_count, factors):
    blk_dev = factors.shape[1] // TILE
    rank = factors.shape[2]
    held = 4 * blk_dev
    slot_total = tile_values.shape[1]
    factor_blocks = factors.reshape(held, TILE, rank)
    layer = (lax.axis_index("tiles") // 2).astype(jnp.int32).reshape(1)
    bf16, f32, i32 = jnp.bfloat16, jnp.float32, jnp.int32

    small = pltpu.CompilerParams(vmem_limit_bytes=8 << 20)
    wanted, slots = pl.pallas_call(
        functools.partial(request_kernel, owners, blk_dev),
        out_shape=(
            pltpu.VMEM((owners, 8, LANES), i32),
            jax.ShapeDtypeStruct((slot_total * 4,), i32),
        ),
        in_specs=[SMEM, SMEM],
        out_specs=(VMEM, SMEM),
        scratch_shapes=[pltpu.SMEM((owners,), i32)],
        name="requests",
    )(tile_coords[0].T, tile_count)
    asked = lax.all_to_all(wanted, "rows", 0, 0)

    narrow, first = pl.pallas_call(
        prepare_kernel,
        out_shape=(pltpu.VMEM(factor_blocks.shape, bf16), pltpu.VMEM(tile_values.shape[2:], bf16)),
        in_specs=[HBM, HBM],
        out_specs=(VMEM, VMEM),
        scratch_shapes=[pltpu.VMEM(factor_blocks.shape, f32), pltpu.SemaphoreType.DMA((2,))],
        compiler_params=small,
        cost_estimate=pl.CostEstimate(flops=0, bytes_accessed=4 << 20, transcendentals=0),
        name="prepare",
    )(in_hbm(factor_blocks), in_hbm(tile_values[0]))
    sent, table = pl.pallas_call(
        functools.partial(serve_kernel, owners),
        out_shape=(
            jax.ShapeDtypeStruct((owners, CAP * TILE, rank), bf16),
            jax.ShapeDtypeStruct((8, LANES), i32),
        ),
        in_specs=[ANY, VMEM],
        out_specs=(ANY, VMEM),
        scratch_shapes=[
            pltpu.SMEM((owners, LANES), i32),
            pltpu.VMEM((owners, CAP * TILE, rank), bf16),
            pltpu.SemaphoreType.DMA((5,)),
        ],
        compiler_params=small,
        name="serve",
    )(in_vmem(asked), in_vmem(narrow))
    blocks = lax.all_to_all(sent, "rows", 0, 0).reshape(owners * CAP * TILE, rank)

    def round_trip(back):
        size = 2 * layers
        return [(i, (i + 2 * back) % size) for i in range(size)]

    tables = [table] + [lax.ppermute(table, "tiles", round_trip(back)) for back in range(1, layers)]

    slots, tables, layer = lax.optimization_barrier((slots, tables, layer))
    flops = 3 * 2 * EDGE * EDGE * rank * slot_total
    messages = pl.pallas_call(
        functools.partial(tile_kernel, owners, layers, 256),
        out_shape=pltpu.VMEM((layers * owners, CAP * TILE // layers, rank), bf16),
        in_specs=[SMEM, SMEM, VMEM, VMEM, HBM],
        out_specs=VMEM,
        scratch_shapes=[
            pltpu.VMEM((slot_total, EDGE, EDGE), bf16),
            pltpu.VMEM((EDGE, EDGE), bf16),
            pltpu.VMEM((EDGE, rank), bf16),
            pltpu.VMEM((EDGE, rank), bf16),
            pltpu.VMEM((owners * CAP, TILE, rank), f32),
            pltpu.SemaphoreType.DMA((slot_total,)),
        ],
        compiler_params=pltpu.CompilerParams(vmem_limit_bytes=32 << 20),
        cost_estimate=pl.CostEstimate(
            flops=flops, bytes_accessed=2 * EDGE * EDGE * slot_total, transcendentals=0
        ),
        name="tiles",
    )(tile_count, slots, in_vmem(blocks), in_vmem(first), in_hbm(tile_values[0]))

    same_core = [
        [t * owners + r for t in range(core, 2 * layers, 2) for r in range(owners)] for core in range(2)
    ]
    came = lax.all_to_all(messages, ("tiles", "rows"), 0, 0, axis_index_groups=same_core)

    height = TILE // layers
    partial = pl.pallas_call(
        functools.partial(add_kernel, owners),
        out_shape=pltpu.VMEM((held * height, rank), bf16),
        in_specs=[SMEM] * (1 + layers) + [VMEM],
        out_specs=VMEM,
        scratch_shapes=[pltpu.VMEM((held, height, rank), f32)] * CAP,
        compiler_params=small,
        name="add",
    )(layer, *tables, in_vmem(came))

    own = [partial] + [lax.ppermute(partial, "tiles", round_trip(back)) for back in range(1, layers)]
    pair = [(i, i ^ 1) for i in range(2 * layers)]
    kept = pl.pallas_call(
        bring_kernel,
        out_shape=pltpu.VMEM(factor_blocks.shape, f32),
        in_specs=[ANY, HBM],
        out_specs=VMEM,
        scratch_shapes=[pltpu.SemaphoreType.DMA],
        compiler_params=small,
        cost_estimate=pl.CostEstimate(flops=0, bytes_accessed=4 << 20, transcendentals=0),
        name="bring",
    )(partial, in_hbm(factor_blocks))
    here, kept = lax.optimization_barrier((partial, kept))
    other = [lax.ppermute(piece, "tiles", pair) for piece in [here] + own[1:]]

    updated = pl.pallas_call(
        update_kernel,
        out_shape=jax.ShapeDtypeStruct(factor_blocks.shape, f32),
        in_specs=[SMEM] + [VMEM] * 9,
        out_specs=ANY,
        scratch_shapes=[pltpu.VMEM(factor_blocks.shape, f32), pltpu.SemaphoreType.DMA((4,))],
        compiler_params=small,
        name="update",
    )(layer, in_vmem(kept), *[in_vmem(piece) for piece in own + other])
    return updated.reshape(factors.shape)


def solution(mesh):
    layers, owners = mesh.shape["tiles"] // 2, mesh.shape["rows"]
    return jax.shard_map(
        functools.partial(on_device, layers, owners),
        mesh=mesh,
        in_specs=(
            P(("tiles", "rows"), None, None, None),
            P(("tiles", "rows"), None, None),
            P(("tiles", "rows")),
            P(None, "rows", None),
        ),
        out_specs=P(None, "rows", None),
        check_vma=False,
    )
```

```python
import functools

import jax
import jax.numpy as jnp
from jax import lax
from jax.experimental import pallas as pl
from jax.experimental.pallas import tpu as pltpu
from jax.sharding import PartitionSpec as P

TILE = 32
CAP = 4
EDGE = TILE * TILE
LANES = 128

step_size = 0.02

VMEM = pl.BlockSpec(memory_space=pltpu.VMEM)
SMEM = pl.BlockSpec(memory_space=pltpu.SMEM)
ANY = pl.BlockSpec(memory_space=pl.ANY)
HBM = pl.BlockSpec(memory_space=pltpu.HBM)


def in_hbm(array):
    return pltpu.with_memory_space_constraint(array, pltpu.HBM)


def in_vmem(array):
    return pltpu.with_memory_space_constraint(array, pltpu.VMEM)


def request_kernel(owners, blk_dev, coords, count, wanted, slots, used):
    lines = (owners, LANES)
    row = lax.broadcasted_iota(jnp.int32, lines, 0)
    lane = lax.broadcasted_iota(jnp.int32, lines, 1)
    for owner in range(owners):
        used[owner] = 0

    def tile(slot, table):
        for mode in range(4):
            block = coords[mode, slot]
            owner = block // blk_dev
            rank = used[owner]
            used[owner] = rank + 1
            slots[slot * 4 + mode] = owner * CAP + rank
            local = mode * blk_dev + block - owner * blk_dev
            table = jnp.where((row == owner) & (lane == rank), local, table)
        return table

    table = lax.fori_loop(0, count[0], tile, jnp.full(lines, -1, jnp.int32))
    for owner in range(owners):
        wanted[owner] = jnp.broadcast_to(table[owner : owner + 1], wanted.shape[1:])


def prepare_kernel(factors, tiles, narrow, first, wide, sems):
    whole = pltpu.make_async_copy(factors, wide, sems.at[0])
    early = pltpu.make_async_copy(tiles.at[0], first, sems.at[1])
    whole.start()
    early.start()
    whole.wait()
    narrow[...] = wide[...].astype(narrow.dtype)
    early.wait()


def bring_kernel(ready, factors, kept, sem):
    del ready
    copy = pltpu.make_async_copy(factors, kept, sem)
    copy.start()
    copy.wait()


def serve_kernel(peers, asked, narrow, sent, table, listed, ready, sems):
    copy = pltpu.make_async_copy(asked.at[:, 0, :], listed, sems.at[0])
    copy.start()
    copy.wait()
    lane = lax.broadcasted_iota(jnp.int32, table.shape, 1)
    line = jnp.full(table.shape, -1, jnp.int32)
    group = peers // 4
    copies = []
    for peer in range(peers):
        for rank in range(CAP):
            local = listed[peer, rank]
            line = jnp.where(lane == peer * CAP + rank, local, line)
            ready[peer, rank * TILE : (rank + 1) * TILE, :] = narrow[jnp.maximum(local, 0)]
        if peer % group == group - 1:
            some = slice(peer + 1 - group, peer + 1)
            copies.append(
                pltpu.make_async_copy(ready.at[some], sent.at[some], sems.at[1 + peer // group])
            )
            copies[-1].start()
    table[...] = line
    for copy in copies:
        copy.wait()


def tile_kernel(
    owners, parts, chunk, count, slots, blocks, early, tiles, out, values, misfit, pair_ab, pair_cd, grads, sems
):
    live, total = count[0], tiles.shape[0]
    f32, bf16 = jnp.float32, jnp.bfloat16
    rank = blocks.shape[-1]

    def fetch(slot):
        return pltpu.make_async_copy(tiles.at[slot], values.at[slot], sems.at[slot])

    for slot in range(1, total):

        @pl.when(slot < live)
        def _():
            fetch(slot).start()

    grads[...] = jnp.zeros_like(grads)

    def tile(slot, tile_at):
        names = [slots[slot * 4 + mode] for mode in range(4)]
        one, two, three, four = [
            blocks[pl.ds(pl.multiple_of(name * TILE, TILE), TILE), :].astype(f32)
            for name in names
        ]
        for i in range(TILE):
            at = slice(i * TILE, (i + 1) * TILE)
            pair_ab[at, :] = (one[i : i + 1] * two).astype(bf16)
            pair_cd[at, :] = (three[i : i + 1] * four).astype(bf16)
        def spread(terms, first, other, kept):
            terms = terms.reshape(-1, TILE, rank)
            for i in range(terms.shape[0]):
                kept = kept + terms[i] * first[i : i + 1]
            return jnp.sum(terms * other[None], axis=1), kept

        def left_of(at, kept):
            left = jnp.dot(misfit[at : at + 2 * chunk, :], pair_cd[...], preferred_element_type=f32)
            return spread(left, one[at // TILE : (at + 2 * chunk) // TILE], two, kept)

        grad_one, grad_two = [], jnp.zeros((TILE, rank), f32)
        for at in range(0, EDGE, 2 * chunk):
            lines = slice(at, at + 2 * chunk)
            model = lax.dot_general(
                pair_ab[lines, :], pair_cd[...], (((1,), (1,)), ((), ())), preferred_element_type=f32
            )
            off = (model - tile_at[lines, :].astype(f32)).astype(bf16)
            misfit[lines, :] = jnp.clip(off, jnp.asarray(-1.0, bf16), jnp.asarray(1.0, bf16))
            if at:
                part_one, grad_two = left_of(at - 2 * chunk, grad_two)
                grad_one.append(part_one)
        part_one, grad_two = left_of(EDGE - 2 * chunk, grad_two)
        grad_one.append(part_one)
        grad_three, grad_four = [], jnp.zeros((TILE, rank), f32)
        for at in range(0, EDGE, chunk):
            right = lax.dot_general(
                misfit[:, at : at + chunk],
                pair_ab[...],
                (((0,), (0,)), ((), ())),
                preferred_element_type=f32,
            )
            first = three[at // TILE : (at + chunk) // TILE]
            part_three, grad_four = spread(right, first, four, grad_four)
            grad_three.append(part_three)
        grads[names[0]] = jnp.concatenate(grad_one, 0)
        grads[names[1]] = grad_two
        grads[names[2]] = jnp.concatenate(grad_three, 0)
        grads[names[3]] = grad_four

    def later(slot, carry):
        fetch(slot).wait()
        tile(slot, values.at[slot])
        return carry

    tile(0, early)
    lax.fori_loop(1, live, later, 0)
    height = TILE // parts
    for owner in range(owners):
        for part in range(parts):
            out[part * owners + owner] = jnp.concatenate(
                [
                    grads[owner * CAP + place, part * height : (part + 1) * height, :]
                    for place in range(CAP)
                ],
                0,
            ).astype(bf16)


def add_kernel(peers, layer, table_0, table_1, table_2, table_3, came, total, *sums):
    tables = (table_0, table_1, table_2, table_3)
    height = total.shape[0] // sums[0].shape[0]
    for acc in sums:
        acc[...] = jnp.zeros_like(acc)
    for back, table in enumerate(tables):
        source = lax.rem(layer[0] + len(tables) - back, len(tables))

        def peer_step(peer, carry, table=table, source=source):
            message = came[source * peers + peer].astype(jnp.float32)
            for rank, acc in enumerate(sums):
                local = jnp.maximum(table[0, peer * CAP + rank], 0)
                acc[local] += message[rank * height : (rank + 1) * height]
            return carry

        lax.fori_loop(0, peers, peer_step, 0, unroll=4)
    summed = sums[0][...] + sums[1][...] + sums[2][...] + sums[3][...]
    total[...] = summed.reshape(total.shape).astype(total.dtype)


def update_kernel(order, layer, factors, *refs):
    own, other, (out, stepped, sems) = refs[:4], refs[4:8], refs[8:]
    parts = len(own)
    height = TILE // parts
    held = factors.shape[0] // 4
    copies = []
    for mode in range(4):
        blocks = slice(mode * held, (mode + 1) * held)
        lines = slice(mode * held * height, (mode + 1) * held * height)
        for back, mine, theirs in zip(order, own, other):
            source = lax.rem(layer[0] + parts - back, parts)
            at = pl.ds(pl.multiple_of(source * height, height), height)
            gradient = mine[lines, :].astype(jnp.float32) + theirs[lines, :].astype(jnp.float32)
            gradient = gradient.reshape(held, height, -1)
            stepped[blocks, at, :] = factors[blocks, at, :] - step_size * gradient
        copies.append(pltpu.make_async_copy(stepped.at[blocks], out.at[blocks], sems.at[mode]))
        copies[-1].start()
    for copy in copies:
        copy.wait()


def on_device(layers, owners, tile_values, tile_coords, tile_count, factors):
    blk_dev = factors.shape[1] // TILE
    rank = factors.shape[2]
    held = 4 * blk_dev
    slot_total = tile_values.shape[1]
    factor_blocks = factors.reshape(held, TILE, rank)
    layer = (lax.axis_index("tiles") // 2).astype(jnp.int32).reshape(1)
    bf16, f32, i32 = jnp.bfloat16, jnp.float32, jnp.int32

    small = pltpu.CompilerParams(vmem_limit_bytes=8 << 20)
    wanted, slots = pl.pallas_call(
        functools.partial(request_kernel, owners, blk_dev),
        out_shape=(
            pltpu.VMEM((owners, 8, LANES), i32),
            jax.ShapeDtypeStruct((slot_total * 4,), i32),
        ),
        in_specs=[SMEM, SMEM],
        out_specs=(VMEM, SMEM),
        scratch_shapes=[pltpu.SMEM((owners,), i32)],
        name="requests",
    )(tile_coords[0].T, tile_count)
    asked = lax.all_to_all(wanted, "rows", 0, 0)

    narrow, first = pl.pallas_call(
        prepare_kernel,
        out_shape=(pltpu.VMEM(factor_blocks.shape, bf16), pltpu.VMEM(tile_values.shape[2:], bf16)),
        in_specs=[HBM, HBM],
        out_specs=(VMEM, VMEM),
        scratch_shapes=[pltpu.VMEM(factor_blocks.shape, f32), pltpu.SemaphoreType.DMA((2,))],
        compiler_params=small,
        cost_estimate=pl.CostEstimate(flops=0, bytes_accessed=4 << 20, transcendentals=0),
        name="prepare",
    )(in_hbm(factor_blocks), in_hbm(tile_values[0]))
    sent, table = pl.pallas_call(
        functools.partial(serve_kernel, owners),
        out_shape=(
            jax.ShapeDtypeStruct((owners, CAP * TILE, rank), bf16),
            jax.ShapeDtypeStruct((8, LANES), i32),
        ),
        in_specs=[ANY, VMEM],
        out_specs=(ANY, VMEM),
        scratch_shapes=[
            pltpu.SMEM((owners, LANES), i32),
            pltpu.VMEM((owners, CAP * TILE, rank), bf16),
            pltpu.SemaphoreType.DMA((5,)),
        ],
        compiler_params=small,
        name="serve",
    )(in_vmem(asked), in_vmem(narrow))
    blocks = lax.all_to_all(sent, "rows", 0, 0).reshape(owners * CAP * TILE, rank)

    def round_trip(back):
        size = 2 * layers
        return [(i, (i + 2 * back) % size) for i in range(size)]

    tables = [table] + [lax.ppermute(table, "tiles", round_trip(back)) for back in range(1, layers)]

    slots, tables, layer = lax.optimization_barrier((slots, tables, layer))
    flops = 3 * 2 * EDGE * EDGE * rank * slot_total
    messages = pl.pallas_call(
        functools.partial(tile_kernel, owners, layers, 256),
        out_shape=pltpu.VMEM((layers * owners, CAP * TILE // layers, rank), bf16),
        in_specs=[SMEM, SMEM, VMEM, VMEM, HBM],
        out_specs=VMEM,
        scratch_shapes=[
            pltpu.VMEM((slot_total, EDGE, EDGE), bf16),
            pltpu.VMEM((EDGE, EDGE), bf16),
            pltpu.VMEM((EDGE, rank), bf16),
            pltpu.VMEM((EDGE, rank), bf16),
            pltpu.VMEM((owners * CAP, TILE, rank), f32),
            pltpu.SemaphoreType.DMA((slot_total,)),
        ],
        compiler_params=pltpu.CompilerParams(vmem_limit_bytes=32 << 20),
        cost_estimate=pl.CostEstimate(
            flops=flops, bytes_accessed=2 * EDGE * EDGE * slot_total, transcendentals=0
        ),
        name="tiles",
    )(tile_count, slots, in_vmem(blocks), in_vmem(first), in_hbm(tile_values[0]))

    same_core = [
        [t * owners + r for t in range(core, 2 * layers, 2) for r in range(owners)] for core in range(2)
    ]
    came = lax.all_to_all(messages, ("tiles", "rows"), 0, 0, axis_index_groups=same_core)

    height = TILE // layers
    partial = pl.pallas_call(
        functools.partial(add_kernel, owners),
        out_shape=pltpu.VMEM((held * height, rank), bf16),
        in_specs=[SMEM] * (1 + layers) + [VMEM],
        out_specs=VMEM,
        scratch_shapes=[pltpu.VMEM((held, height, rank), f32)] * CAP,
        compiler_params=small,
        name="add",
    )(layer, *tables, in_vmem(came))

    order = [0] + sorted(range(1, layers), key=lambda back: -min(back, layers - back))
    own = [partial] + [lax.ppermute(partial, "tiles", round_trip(back)) for back in order[1:]]
    pair = [(i, i ^ 1) for i in range(2 * layers)]
    kept = pl.pallas_call(
        bring_kernel,
        out_shape=pltpu.VMEM(factor_blocks.shape, f32),
        in_specs=[ANY, HBM],
        out_specs=VMEM,
        scratch_shapes=[pltpu.SemaphoreType.DMA],
        compiler_params=small,
        cost_estimate=pl.CostEstimate(flops=0, bytes_accessed=4 << 20, transcendentals=0),
        name="bring",
    )(partial, in_hbm(factor_blocks))
    here, kept = lax.optimization_barrier((partial, kept))
    other = [lax.ppermute(piece, "tiles", pair) for piece in [here] + own[1:]]

    updated = pl.pallas_call(
        functools.partial(update_kernel, order),
        out_shape=jax.ShapeDtypeStruct(factor_blocks.shape, f32),
        in_specs=[SMEM] + [VMEM] * 9,
        out_specs=ANY,
        scratch_shapes=[pltpu.VMEM(factor_blocks.shape, f32), pltpu.SemaphoreType.DMA((4,))],
        compiler_params=small,
        name="update",
    )(layer, in_vmem(kept), *[in_vmem(piece) for piece in own + other])
    return updated.reshape(factors.shape)


def solution(mesh):
    layers, owners = mesh.shape["tiles"] // 2, mesh.shape["rows"]
    return jax.shard_map(
        functools.partial(on_device, layers, owners),
        mesh=mesh,
        in_specs=(
            P(("tiles", "rows"), None, None, None),
            P(("tiles", "rows"), None, None),
            P(("tiles", "rows")),
            P(None, "rows", None),
        ),
        out_specs=P(None, "rows", None),
        check_vma=False,
    )
```
